512 devices in a mesh: rows: 64 (over z, y), cols: 8 (over x, core).
Axes of the slice: x: 4, y: 4, z: 16, core: 2. Of those that a mesh axis runs over, the one named last changes fastest.
Arguments:
- noise: bfloat16 [16384, 4096], P('rows', 'cols'), may hold values from -8 to 8
- data: bfloat16 [4096, 4096], P('cols', 'rows'), may hold values from -8 to 8
Outputs:
- targets: bfloat16 [16384, 4096], P('rows', 'cols')
The draws below stay inside these ranges and needn't reach their ends.
All inputs are finite; a program needn't handle non-finite values.
Results may differ from the reference program's by a relative error of at most 0.017.
Values may be sent and summed in bfloat16 or wider, within the bound.
A program may use at most 64 MiB of HBM per device.

```python
import math
import jax
import jax.numpy as jnp
from jax import lax

FEATURES = 4096
SWEEPS = 3
NOISE_ROWS = 16384
DATA_ROWS = 4096


def paired_rows(key):
    center = jax.random.normal(jax.random.fold_in(key, 91), (FEATURES,), jnp.float32)
    base = jax.random.normal(key, (DATA_ROWS, FEATURES), jnp.float32)
    even_rows = base[0::2]
    odd_rows = base[1::2]
    stacked = jnp.stack([even_rows, odd_rows], axis=1).reshape(DATA_ROWS, FEATURES)
    far_key = jax.random.fold_in(key, 53)
    offsets = jax.random.randint(jax.random.fold_in(far_key, 1), (DATA_ROWS // 32,), 0, 32)
    index = jnp.arange(DATA_ROWS)
    far_mask = index % 32 == jnp.repeat(offsets, 32)
    signs = jnp.where(jax.random.bernoulli(jax.random.fold_in(far_key, 2), 0.5, (DATA_ROWS,)), 1.0, -1.0)
    far_rows = signs[:, None] * (4.0 + 0.5 * jax.random.normal(jax.random.fold_in(far_key, 3), (DATA_ROWS, FEATURES), jnp.float32))
    stacked = jnp.where(far_mask[:, None], far_rows, stacked + center[None, :])
    return jnp.clip(stacked, -8.0, 8.0)


def draw_noise(key, part):
    key = jax.random.fold_in(key, 3)
    values = jax.random.normal(key, (NOISE_ROWS, FEATURES), jnp.float32)
    index = jnp.arange(NOISE_ROWS)
    far_key = jax.random.fold_in(key, 61)
    offsets = jax.random.randint(jax.random.fold_in(far_key, 1), (NOISE_ROWS // 64,), 1, 32)
    far_mask = index % 64 == jnp.repeat(offsets, 64)
    signs = jnp.where(jax.random.bernoulli(jax.random.fold_in(far_key, 2), 0.5, (NOISE_ROWS, FEATURES)), 1.0, -1.0)
    far_rows = signs * (4.0 + 0.5 * jax.random.normal(jax.random.fold_in(far_key, 3), (NOISE_ROWS, FEATURES), jnp.float32))
    values = jnp.where(far_mask[:, None], far_rows, values)
    return jnp.clip(values, -8.0, 8.0).astype(jnp.bfloat16)


def draw_data(key, part):
    shared = key
    values = paired_rows(shared)
    return jnp.clip(values, -8.0, 8.0).astype(jnp.bfloat16)


def setup_inputs(seed: int = 0) -> dict:
    seeds = jax.random.split(jax.random.key(seed), 3)
    noise = draw_noise(jax.random.fold_in(seeds[2], 71), 0)
    data = draw_data(jax.random.fold_in(seeds[2], 71), 0)
    return {"noise": noise, "data": data}


epsilon = 1.0

def reference(noise, data):
    noise_sq = lax.optimization_barrier(jnp.sum(jnp.square(noise.astype(jnp.float32)), axis=1))
    data_sq = lax.optimization_barrier(jnp.sum(jnp.square(data.astype(jnp.float32)), axis=1))
    products = jnp.dot(noise, data.T, preferred_element_type=jnp.float32)
    distance = (noise_sq[:, None] + data_sq[None, :] - 2.0 * products) / math.sqrt(FEATURES)
    dual_cols = jnp.zeros((DATA_ROWS,), jnp.float32)
    dual_rows = jnp.zeros((NOISE_ROWS,), jnp.float32)
    for sweep_index in range(SWEEPS):
        dual_rows = -epsilon * math.log(NOISE_ROWS) - epsilon * jax.nn.logsumexp((dual_cols[None, :] - distance) / epsilon, axis=1)
        dual_cols = -epsilon * math.log(DATA_ROWS) - epsilon * jax.nn.logsumexp((dual_rows[:, None] - distance) / epsilon, axis=0)
    weights = jnp.exp((dual_rows[:, None] + dual_cols[None, :] - distance) / epsilon + math.log(NOISE_ROWS))
    row_totals = lax.optimization_barrier(jnp.sum(weights, axis=1))
    coupling = weights.astype(jnp.bfloat16)
    numerators = jnp.dot(coupling, data, preferred_element_type=jnp.float32)
    return (numerators / row_totals[:, None]).astype(jnp.bfloat16)
```

```python
import math

import jax
import jax.numpy as jnp
from jax import lax
from jax.experimental import pallas as pl
from jax.experimental.pallas import tpu as pltpu
from jax.sharding import PartitionSpec as P

FEATURES = 4096
NY = 4
NX = 4
F32 = jnp.float32
BF16 = jnp.bfloat16
NT = (((1,), (1,)), ((), ()))
PART_A = 16


def kernel(
    nz, noise_ref, data_ref, out_ref,
    gathered, noise_all, dist, row_box, col_y, col_z, sib_out, sib_in, pair, relay, inbox, own,
    recv_a, recv_b, recv_q, recv_n, recv_row, recv_y, recv_z, recv_sib, recv_relay, recv_in,
    send_a, send_b, send_ya, send_yb, send_q, send_n, send_row, send_y, send_z, send_sib, send_x,
):
    nc = 2 * NX
    rows, feats = noise_ref.shape
    dcols, depth = data_ref.shape
    part_b = depth - PART_A
    half = dcols // 2
    fhalf = feats // 2
    log_noise = math.log(rows * nz * NY)
    log_data = math.log(dcols * nc)

    me_r, me_c = lax.axis_index("rows"), lax.axis_index("cols")
    z, y = me_r // NY, lax.rem(me_r, NY)
    x, core = me_c // 2, lax.rem(me_c, 2)

    def at_z(k):
        return (lax.rem(z + k + nz, nz) * NY + y, me_c)

    def at_y(k):
        return (z * NY + lax.rem(y + k + NY, NY), me_c)

    def at_c(k):
        return (me_r, lax.rem(me_c + k + nc, nc))

    def at_x(k):
        return (me_r, lax.rem(x + k + NX, NX) * 2 + core)

    sibling = (me_r, x * 2 + 1 - core)

    def send(src, dst, send_sem, recv_sem, device):
        pltpu.make_async_remote_copy(
            src_ref=src, dst_ref=dst, send_sem=send_sem, recv_sem=recv_sem,
            device_id=device, device_id_type=pl.DeviceIdType.MESH,
        ).start()

    def wait(ref, sem):
        pltpu.make_async_copy(ref, ref, sem).wait()

    barrier = pltpu.get_barrier_semaphore()
    partners = (
        [at_z(k) for k in range(1, nz)] + [at_y(k) for k in range(1, NY)] + [at_c(k) for k in range(1, nc)]
    )
    for device in partners:
        pl.semaphore_signal(barrier, inc=1, device_id=device, device_id_type=pl.DeviceIdType.MESH)

    def chunk_a(chunk):
        return gathered.at[pl.ds(pl.multiple_of(chunk * depth, 16), PART_A)]

    def chunk_b(chunk):
        return gathered.at[pl.ds(pl.multiple_of(chunk * depth + PART_A, 16), part_b)]

    def chunk_q(chunk, q):
        return gathered.at[pl.ds(pl.multiple_of(chunk * depth + PART_A, 16), part_b), q * half:(q + 1) * half]

    gathered[pl.ds(pl.multiple_of(me_r * depth, 16), depth), :] = jnp.transpose(data_ref[...].astype(F32)).astype(BF16)
    noise_all[me_c] = noise_ref[...]

    pl.semaphore_wait(barrier, len(partners))

    mine = noise_all.at[me_c]
    for k in (1, 3, 2):
        send(mine, mine, send_n, recv_n.at[me_c], at_x(k))
    send(mine, mine, send_n, recv_n.at[me_c], sibling)

    b = chunk_b(me_r)
    a = chunk_a(me_r)
    for k in (1, -1):
        send(b, b, send_b, recv_b.at[me_r], at_z(k))
    for k in (1, 3, 2):
        send(a, a, send_ya, recv_a.at[me_r], at_y(k))
    for k in (1, -1):
        send(a, a, send_a, recv_a.at[me_r], at_z(k))
    for k in (1, -1):
        send(b, b, send_yb, recv_b.at[me_r], at_y(k))
    for k in range(1, NY):
        chunk = z * NY + lax.rem(y + k, NY)
        a = chunk_a(chunk)
        wait(a, recv_a.at[chunk])
        for d in (1, -1):
            send(a, a, send_a, recv_a.at[chunk], at_z(d))

    def along_z(step, d, forward):
        z0 = lax.rem(z - d * step + nz, nz)
        chunk = z0 * NY + y
        ref = chunk_b(chunk)
        wait(ref, recv_b.at[chunk])
        if forward:
            send(ref, ref, send_b, recv_b.at[chunk], at_z(d))
        for k in (1, -1):
            send(ref, ref, send_yb, recv_b.at[chunk], at_y(k))
        for k in range(NY):
            chunk = z0 * NY + lax.rem(y + k, NY)
            ref = chunk_a(chunk)
            wait(ref, recv_a.at[chunk])
            if forward:
                send(ref, ref, send_a, recv_a.at[chunk], at_z(d))

    def along_y(z0):
        for q, d in ((0, 1), (1, -1)):
            chunk = z0 * NY + lax.rem(y - d + NY, NY)
            wait(chunk_b(chunk), recv_b.at[chunk])
            ref = chunk_q(chunk, q)
            send(ref, ref, send_q, recv_q.at[z0 * 2 + q], at_y(d))

    def noise_relay():
        for k in (1, 3, 2):
            c = lax.rem(x + k, NX) * 2 + core
            ref = noise_all.at[c]
            wait(ref, recv_n.at[c])
            send(ref, ref, send_n, recv_n.at[c], sibling)

    last = nz // 2
    along_z(1, 1, True)
    along_z(1, -1, True)
    along_y(z)

    def gather_step(step, carry):
        along_z(step, 1, True)
        along_z(step, -1, True)
        along_y(lax.rem(z - (step - 1) + nz, nz))
        along_y(lax.rem(z + (step - 1), nz))
        return carry

    lax.fori_loop(2, 5, gather_step, 0)
    noise_relay()
    lax.fori_loop(5, last - 1, gather_step, 0)
    along_z(last - 1, 1, True)
    along_z(last - 1, -1, False)
    along_y(lax.rem(z - (last - 2) + nz, nz))
    along_y(lax.rem(z + (last - 2), nz))
    along_z(last, 1, False)
    along_y(lax.rem(z - (last - 1) + nz, nz))
    along_y(lax.rem(z + (last - 1), nz))
    along_y(lax.rem(z + last, nz))

    def across(z0, carry):
        chunk = z0 * NY + lax.rem(y + 2, NY)
        for q in (0, 1):
            wait(chunk_q(chunk, q), recv_q.at[z0 * 2 + q])
        return carry

    lax.fori_loop(0, nz, across, 0)
    for k in range(NX):
        c = lax.rem(x + k, NX) * 2 + 1 - core
        wait(noise_all.at[c], recv_n.at[c])

    dist[...] = jnp.zeros_like(dist)

    def product_step(c, carry):
        noise_sq, data_sq = carry
        n = noise_all[c]
        d = gathered[pl.ds(pl.multiple_of(c * feats, 16), feats), :]
        dist[...] += jnp.dot(n, d, preferred_element_type=F32)
        n, d = n.astype(F32), d.astype(F32)
        return (
            noise_sq + jnp.sum(n * n, axis=1, keepdims=True),
            data_sq + jnp.sum(d * d, axis=0, keepdims=True),
        )

    noise_sq, data_sq = lax.fori_loop(
        0, nc, product_step, (jnp.zeros((rows, 1), F32), jnp.zeros((1, dcols), F32))
    )
    dist[...] = (noise_sq + data_sq - 2.0 * dist[...]) / math.sqrt(FEATURES)

    def to_lanes(column):
        return jnp.transpose(jnp.broadcast_to(column, (rows, 128)))[0:1, :]

    def to_column(lanes):
        return jnp.transpose(jnp.broadcast_to(lanes, (128, rows)))[:, 0:1]

    def exchange(box, it, value, send_sem, recv_sem, count, place):
        box[it, 0] = value
        for k in range(1, count):
            send(box.at[it, 0], box.at[it, count - k], send_sem.at[it], recv_sem.at[it], place(k))
        wait(box.at[it, pl.ds(1, count - 1)], recv_sem.at[it])
        return box[it]

    def logsum(parts):
        top = jnp.max(parts, axis=0)
        return top + jnp.log(jnp.sum(jnp.exp(parts - top), axis=0))

    def over_cols(it, value):
        return exchange(row_box, it, value, send_row, recv_row, nc, at_c)

    scores = -dist[...]
    top = jnp.max(scores, axis=1, keepdims=True)
    logs = top + jnp.log(jnp.sum(jnp.exp(scores - top), axis=1, keepdims=True))
    u = to_column(-log_noise - logsum(over_cols(0, to_lanes(logs))))

    scores = u - dist[...]
    top = jnp.max(scores, axis=0, keepdims=True)
    logs = top + jnp.log(jnp.sum(jnp.exp(scores - top), axis=0, keepdims=True))
    logs = logsum(exchange(col_y, 0, logs, send_y, recv_y, NY, at_y))
    v = -log_data - logsum(exchange(col_z, 0, logs, send_z, recv_z, nz, at_z))

    for it in (1, 2):
        total = jnp.sum(jnp.exp(u + v - dist[...]), axis=1, keepdims=True)
        total = jnp.sum(over_cols(it, to_lanes(total)), axis=0)
        u = u - to_column(log_noise + jnp.log(total))
        total = jnp.sum(jnp.exp(u + v - dist[...]), axis=0, keepdims=True)
        total = jnp.sum(exchange(col_y, it, total, send_y, recv_y, NY, at_y), axis=0)
        total = jnp.sum(exchange(col_z, it, total, send_z, recv_z, nz, at_z), axis=0)
        v = v - (log_data + jnp.log(total))

    weights = jnp.exp(u + v - dist[...] + log_noise)
    row_box[3, 0] = to_lanes(jnp.sum(weights, axis=1, keepdims=True))
    for k in range(1, nc):
        send(row_box.at[3, 0], row_box.at[3, nc - k], send_row.at[3], recv_row.at[3], at_c(k))
    coupling = weights.astype(BF16)

    def share(c):
        d = gathered[pl.ds(pl.multiple_of(c * feats, 16), feats), :]
        return lax.dot_general(coupling, d, NT, preferred_element_type=F32)

    for k in (2, 1, 3, 0):
        sib_out[k] = share(lax.rem(x + k, NX) * 2 + 1 - core).astype(BF16)
        send(sib_out.at[k], sib_in.at[k], send_sib, recv_sib.at[k], sibling)

    def both(k):
        block = share(lax.rem(x + k, NX) * 2 + core)
        wait(sib_in.at[k], recv_sib.at[k])
        return block + sib_in[k].astype(F32)

    block = both(2)
    pair[2] = block[:, :fhalf].astype(BF16)
    pair[5] = block[:, fhalf:].astype(BF16)
    send(pair.at[2], relay.at[0], send_x, recv_relay.at[0], at_x(1))
    send(pair.at[5], relay.at[1], send_x, recv_relay.at[1], at_x(-1))
    right = both(1)
    pair[1] = right[:, fhalf:].astype(BF16)
    send(pair.at[1], inbox.at[1], send_x, recv_in.at[1], at_x(1))
    left = both(3)
    pair[3] = left[:, :fhalf].astype(BF16)
    send(pair.at[3], inbox.at[2], send_x, recv_in.at[2], at_x(-1))
    wait(relay.at[0], recv_relay.at[0])
    pair[0] = (right[:, :fhalf] + relay[0].astype(F32)).astype(BF16)
    send(pair.at[0], inbox.at[0], send_x, recv_in.at[0], at_x(1))
    wait(relay.at[1], recv_relay.at[1])
    pair[4] = (left[:, fhalf:] + relay[1].astype(F32)).astype(BF16)
    send(pair.at[4], inbox.at[3], send_x, recv_in.at[3], at_x(-1))
    own[...] = both(0)
    wait(row_box.at[3, pl.ds(1, nc - 1)], recv_row.at[3])
    totals = to_column(jnp.sum(row_box[3], axis=0))
    for i in (1, 2, 0, 3):
        wait(inbox.at[i], recv_in.at[i])
    low = own[:, :fhalf] + inbox[0].astype(F32) + inbox[2].astype(F32)
    high = own[:, fhalf:] + inbox[1].astype(F32) + inbox[3].astype(F32)
    out_ref[:, :fhalf] = (low / totals).astype(BF16)
    out_ref[:, fhalf:] = (high / totals).astype(BF16)

    hops = nz - 1
    wait(gathered.at[pl.ds(0, hops * NY * PART_A)], send_a)
    wait(gathered.at[pl.ds(0, hops * part_b)], send_b)
    wait(gathered.at[pl.ds(0, 3 * PART_A)], send_ya)
    wait(gathered.at[pl.ds(0, 2 * nz * part_b)], send_yb)
    wait(gathered.at[pl.ds(0, nz * part_b)], send_q)
    wait(noise_all.at[pl.ds(0, nc - 1)], send_n)
    for it in range(4):
        wait(row_box.at[it, pl.ds(1, nc - 1)], send_row.at[it])
    for it in range(3):
        wait(col_y.at[it, pl.ds(1, NY - 1)], send_y.at[it])
        wait(col_z.at[it, pl.ds(1, nz - 1)], send_z.at[it])
    wait(sib_out, send_sib)
    wait(pair, send_x)


def solution(mesh):
    nz = mesh.shape["rows"] // NY
    nc = mesh.shape["cols"]

    def shards(noise, data):
        rows, feats = noise.shape
        dcols, depth = data.shape
        dma = pltpu.SemaphoreType.DMA
        vmem = pl.BlockSpec(memory_space=pltpu.VMEM)

        def body(*refs):
            kernel(nz, *refs)

        return pl.pallas_call(
            body,
            out_shape=jax.ShapeDtypeStruct((rows, feats), BF16),
            in_specs=[vmem] * 2,
            out_specs=vmem,
            scratch_shapes=[
                pltpu.VMEM((FEATURES, dcols), BF16),
                pltpu.VMEM((nc, rows, feats), BF16),
                pltpu.VMEM((rows, dcols), F32),
                pltpu.VMEM((4, nc, 1, rows), F32),
                pltpu.VMEM((3, NY, 1, dcols), F32),
                pltpu.VMEM((3, nz, 1, dcols), F32),
                pltpu.VMEM((NX, rows, feats), BF16),
                pltpu.VMEM((NX, rows, feats), BF16),
                pltpu.VMEM((6, rows, feats // 2), BF16),
                pltpu.VMEM((2, rows, feats // 2), BF16),
                pltpu.VMEM((4, rows, feats // 2), BF16),
                pltpu.VMEM((rows, feats), F32),
                dma((nz * NY,)), dma((nz * NY,)), dma((nz * 2,)), dma((nc,)),
                dma((4,)), dma((3,)), dma((3,)), dma((NX,)), dma((2,)), dma((4,)),
                dma, dma, dma, dma, dma, dma, dma((4,)), dma((3,)), dma((3,)), dma, dma,
            ],
            compiler_params=pltpu.CompilerParams(
                collective_id=0, has_side_effects=True, vmem_limit_bytes=40 * 2**20
            ),
        )(noise, data)

    return jax.shard_map(
        shards,
        mesh=mesh,
        in_specs=(P("rows", "cols"), P("cols", "rows")),
        out_specs=P("rows", "cols"),
        check_vma=False,
    )
```

```python
import math

import jax
import jax.numpy as jnp
from jax import lax
from jax.experimental import pallas as pl
from jax.experimental.pallas import tpu as pltpu
from jax.sharding import PartitionSpec as P

FEATURES = 4096
NY = 4
NX = 4
F32 = jnp.float32
BF16 = jnp.bfloat16
NT = (((1,), (1,)), ((), ()))
PART_A = 16


def kernel(
    nz, noise_ref, data_ref, out_ref,
    gathered, noise_all, dist, square, row_box, col_y, col_z, sib_out, sib_in, pair, relay, inbox, own,
    local, recv_a, recv_b, recv_q, recv_n, recv_row, recv_y, recv_z, recv_sib, recv_relay, recv_in,
    send_a, send_b, send_ya, send_yb, send_q, send_n, send_row, send_y, send_z, send_sib, send_x,
):
    nc = 2 * NX
    rows, feats = noise_ref.shape
    depth, dcols = data_ref.shape
    part_b = depth - PART_A
    half = dcols // 2
    fhalf = feats // 2
    log_noise = math.log(rows * nz * NY)
    log_data = math.log(dcols * nc)

    me_r, me_c = lax.axis_index("rows"), lax.axis_index("cols")
    z, y = me_r // NY, lax.rem(me_r, NY)
    x, core = me_c // 2, lax.rem(me_c, 2)

    def at_z(k):
        return (lax.rem(z + k + nz, nz) * NY + y, me_c)

    def at_y(k):
        return (z * NY + lax.rem(y + k + NY, NY), me_c)

    def at_c(k):
        return (me_r, lax.rem(me_c + k + nc, nc))

    def at_x(k):
        return (me_r, lax.rem(x + k + NX, NX) * 2 + core)

    sibling = (me_r, x * 2 + 1 - core)

    def send(src, dst, send_sem, recv_sem, device):
        pltpu.make_async_remote_copy(
            src_ref=src, dst_ref=dst, send_sem=send_sem, recv_sem=recv_sem,
            device_id=device, device_id_type=pl.DeviceIdType.MESH,
        ).start()

    def wait(ref, sem):
        pltpu.make_async_copy(ref, ref, sem).wait()

    barrier = pltpu.get_barrier_semaphore()
    partners = [at_z(1), at_z(-1), sibling] + [at_y(k) for k in range(1, NY)] + [at_x(k) for k in range(1, NX)]
    for device in partners:
        pl.semaphore_signal(barrier, inc=1, device_id=device, device_id_type=pl.DeviceIdType.MESH)

    def chunk_a(chunk):
        return gathered.at[pl.ds(pl.multiple_of(chunk * depth, 16), PART_A)]

    def chunk_b(chunk, p):
        return gathered.at[pl.ds(pl.multiple_of(chunk * depth + PART_A, 16), part_b), p * half:(p + 1) * half]

    keep_data = pltpu.make_async_copy(
        data_ref, gathered.at[pl.ds(pl.multiple_of(me_r * depth, 16), depth)], local.at[0])
    keep_noise = pltpu.make_async_copy(noise_ref, noise_all.at[me_c], local.at[1])
    keep_data.start()
    keep_noise.start()
    pl.semaphore_wait(barrier, len(partners))

    my_a = data_ref.at[pl.ds(0, PART_A)]
    a = chunk_a(me_r)
    for p in (0, 1):
        my_b = data_ref.at[pl.ds(PART_A, part_b), p * half:(p + 1) * half]
        for d in (1, -1):
            send(my_b, chunk_b(me_r, p), send_b, recv_b.at[me_r * 2 + p], at_z(d))
    for k in (1, 3, 2):
        send(my_a, a, send_ya, recv_a.at[me_r], at_y(k))
    for d in (1, -1):
        send(my_a, a, send_a, recv_a.at[me_r], at_z(d))
    for p in (0, 1):
        my_b = data_ref.at[pl.ds(PART_A, part_b), p * half:(p + 1) * half]
        for d in (1, -1):
            send(my_b, chunk_b(me_r, p), send_yb, recv_b.at[me_r * 2 + p], at_y(d))

    mine = noise_all.at[me_c]
    for k in (1, 3, 2):
        send(noise_ref, mine, send_n, recv_n.at[me_c], at_x(k))
    send(noise_ref, mine, send_n, recv_n.at[me_c], sibling)

    def plane(step):
        return lax.rem(z + step + nz, nz)

    def part_a(step, k, ways):
        chunk = plane(-step) * NY + lax.rem(y + k, NY)
        ref = chunk_a(chunk)
        wait(ref, recv_a.at[chunk])
        for d in ways:
            send(ref, ref, send_a, recv_a.at[chunk], at_z(d))

    def part_b_z(p, step, ways):
        chunk = plane(-step) * NY + y
        ref, sem = chunk_b(chunk, p), recv_b.at[chunk * 2 + p]
        wait(ref, sem)
        for d in ways:
            send(ref, ref, send_b, sem, at_z(d))
        for d in (1, -1):
            send(ref, ref, send_yb, sem, at_y(d))

    def part_b_y(p, step):
        d = 1 - 2 * p
        z0 = plane(-step)
        chunk = z0 * NY + lax.rem(y - d + NY, NY)
        ref = chunk_b(chunk, p)
        wait(ref, recv_b.at[chunk * 2 + p])
        send(ref, ref, send_q, recv_q.at[z0 * 2 + p], at_y(d))

    def gather_step(step, ends, befores):
        for p in (0, 1):
            for s, ways in ends:
                part_b_z(p, s, ways)
            for s, ways in befores:
                part_b_y(p, s)
        for k in (3, 1):
            for s, ways in befores:
                part_a(s, k, ways)
        for s, ways in ends:
            part_a(s, 0, ways)
        for s, ways in befores:
            part_a(s, 2, ways)

    last = nz // 2
    both = (1, -1)

    def inner_step(step, carry):
        gather_step(step, ((step, (1,)), (-step, (-1,))), ((step - 1, (1,)), (1 - step, (-1,))))
        return carry

    for p in (0, 1):
        for d in both:
            part_b_z(p, d, (d,))
    for k in (3, 1):
        part_a(0, k, both)
    for p in (0, 1):
        part_b_y(p, 0)
    for d in both:
        part_a(d, 0, (d,))
    part_a(0, 2, both)
    lax.fori_loop(2, last - 3, inner_step, 0)
    for k in (1, 3, 2):
        c = lax.rem(x + k, NX) * 2 + core
        ref = noise_all.at[c]
        wait(ref, recv_n.at[c])
        send(ref, ref, send_n, recv_n.at[c], sibling)
    inner_step(last - 3, 0)
    for k in range(NX):
        c = lax.rem(x + k, NX) * 2 + 1 - core
        wait(noise_all.at[c], recv_n.at[c])
    keep_data.wait()
    keep_noise.wait()

    width = NY * depth

    def noise_step(c, total):
        n = noise_all[c].astype(F32)
        return total + jnp.sum(n * n, axis=1, keepdims=True)

    noise_sq = lax.fori_loop(0, nc, noise_step, jnp.zeros((rows, 1), F32))
    square[...] = jnp.zeros_like(square)
    dist[...] = jnp.zeros_like(dist)

    def arrived(z0):
        left, right, across = (z0 * NY + lax.rem(y + k, NY) for k in (3, 1, 2))
        wait(chunk_b(left, 1), recv_b.at[left * 2 + 1])
        wait(chunk_b(right, 0), recv_b.at[right * 2])
        for p in (0, 1):
            wait(chunk_b(across, p), recv_q.at[z0 * 2 + p])

    def product(step):
        z0 = plane(step)
        arrived(z0)
        d = gathered[pl.ds(pl.multiple_of(z0 * width, 16), width), :]
        first = pl.multiple_of(lax.rem(z0, feats // width) * width, width)
        n = noise_all[z0 // (feats // width), :, pl.ds(first, width)]
        dist[...] += jnp.dot(n, d, preferred_element_type=F32)
        d = d.astype(F32)
        square[...] += jnp.sum(d * d, axis=0, keepdims=True)

    def products(first, stop):
        def step(i, carry):
            product(first + i)
            return carry

        lax.fori_loop(0, stop - first, step, 0)

    products(-1, 2)
    inner_step(last - 2, 0)
    products(-3, -1)
    products(2, 4)
    s = last - 1
    gather_step(s, ((s, (1,)), (-s, ())), ((s - 1, (1,)), (1 - s, (-1,))))
    products(1 - s + 1, -3)
    products(4, s - 1)
    gather_step(last, ((last, ()),), ((s, (1,)), (-s, ())))
    products(1 - s, 2 - s)
    products(s - 1, s)
    for p in (0, 1):
        part_b_y(p, last)
    for k in (3, 1, 2):
        part_a(last, k, ())
    products(-s, 1 - s)
    products(s, last + 1)
    dist[...] = (noise_sq + square[...] - 2.0 * dist[...]) / math.sqrt(FEATURES)

    def to_lanes(column):
        return jnp.transpose(jnp.broadcast_to(column, (rows, 128)))[0:1, :]

    def to_column(lanes):
        return jnp.transpose(jnp.broadcast_to(lanes, (128, rows)))[:, 0:1]

    def exchange(box, it, value, send_sem, recv_sem, count, place):
        box[it, 0] = value
        for k in sorted(range(1, count), key=lambda k: -min(k, count - k)):
            send(box.at[it, 0], box.at[it, count - k], send_sem.at[it], recv_sem.at[it], place(k))
        wait(box.at[it, pl.ds(1, count - 1)], recv_sem.at[it])
        return box[it]

    def logsum(parts):
        top = jnp.max(parts, axis=0)
        return top + jnp.log(jnp.sum(jnp.exp(parts - top), axis=0))

    def over_cols(it, value):
        return exchange(row_box, it, value, send_row, recv_row, nc, at_c)

    scores = -dist[...]
    top = jnp.max(scores, axis=1, keepdims=True)
    logs = top + jnp.log(jnp.sum(jnp.exp(scores - top), axis=1, keepdims=True))
    u = to_column(-log_noise - logsum(over_cols(0, to_lanes(logs))))

    scores = u - dist[...]
    top = jnp.max(scores, axis=0, keepdims=True)
    logs = top + jnp.log(jnp.sum(jnp.exp(scores - top), axis=0, keepdims=True))
    logs = logsum(exchange(col_y, 0, logs, send_y, recv_y, NY, at_y))
    v = -log_data - logsum(exchange(col_z, 0, logs, send_z, recv_z, nz, at_z))

    for it in (1, 2):
        total = jnp.sum(jnp.exp(u + v - dist[...]), axis=1, keepdims=True)
        total = jnp.sum(over_cols(it, to_lanes(total)), axis=0)
        u = u - to_column(log_noise + jnp.log(total))
        total = jnp.sum(jnp.exp(u + v - dist[...]), axis=0, keepdims=True)
        total = jnp.sum(exchange(col_y, it, total, send_y, recv_y, NY, at_y), axis=0)
        total = jnp.sum(exchange(col_z, it, total, send_z, recv_z, nz, at_z), axis=0)
        v = v - (log_data + jnp.log(total))

    weights = jnp.exp(u + v - dist[...] + log_noise)
    row_box[3, 0] = to_lanes(jnp.sum(weights, axis=1, keepdims=True))
    for k in range(1, nc):
        send(row_box.at[3, 0], row_box.at[3, nc - k], send_row.at[3], recv_row.at[3], at_c(k))
    coupling = weights.astype(BF16)

    def share(c):
        d = gathered[pl.ds(pl.multiple_of(c * feats, 16), feats), :]
        return lax.dot_general(coupling, d, NT, preferred_element_type=F32)

    for k in (2, 1, 3, 0):
        sib_out[k] = share(lax.rem(x + k, NX) * 2 + 1 - core).astype(BF16)
        send(sib_out.at[k], sib_in.at[k], send_sib, recv_sib.at[k], sibling)

    def both(k):
        block = share(lax.rem(x + k, NX) * 2 + core)
        wait(sib_in.at[k], recv_sib.at[k])
        return block + sib_in[k].astype(F32)

    block = both(2)
    pair[2] = block[:, :fhalf].astype(BF16)
    pair[5] = block[:, fhalf:].astype(BF16)
    send(pair.at[2], relay.at[0], send_x, recv_relay.at[0], at_x(1))
    send(pair.at[5], relay.at[1], send_x, recv_relay.at[1], at_x(-1))
    right = both(1)
    pair[1] = right[:, fhalf:].astype(BF16)
    send(pair.at[1], inbox.at[1], send_x, recv_in.at[1], at_x(1))
    left = both(3)
    pair[3] = left[:, :fhalf].astype(BF16)
    send(pair.at[3], inbox.at[2], send_x, recv_in.at[2], at_x(-1))
    wait(relay.at[0], recv_relay.at[0])
    pair[0] = (right[:, :fhalf] + relay[0].astype(F32)).astype(BF16)
    send(pair.at[0], inbox.at[0], send_x, recv_in.at[0], at_x(1))
    wait(relay.at[1], recv_relay.at[1])
    pair[4] = (left[:, fhalf:] + relay[1].astype(F32)).astype(BF16)
    send(pair.at[4], inbox.at[3], send_x, recv_in.at[3], at_x(-1))
    own[...] = both(0)
    wait(row_box.at[3, pl.ds(1, nc - 1)], recv_row.at[3])
    totals = to_column(jnp.sum(row_box[3], axis=0))
    for i in (1, 2, 0, 3):
        wait(inbox.at[i], recv_in.at[i])
    low = own[:, :fhalf] + inbox[0].astype(F32) + inbox[2].astype(F32)
    high = own[:, fhalf:] + inbox[1].astype(F32) + inbox[3].astype(F32)
    out_ref[:, :fhalf] = (low / totals).astype(BF16)
    out_ref[:, fhalf:] = (high / totals).astype(BF16)

    hops = nz - 1
    wait(gathered.at[pl.ds(0, hops * NY * PART_A)], send_a)
    wait(gathered.at[pl.ds(0, hops * part_b)], send_b)
    wait(gathered.at[pl.ds(0, 3 * PART_A)], send_ya)
    wait(gathered.at[pl.ds(0, 2 * nz * part_b)], send_yb)
    wait(gathered.at[pl.ds(0, nz * part_b)], send_q)
    wait(noise_all.at[pl.ds(0, nc - 1)], send_n)
    for it in range(4):
        wait(row_box.at[it, pl.ds(1, nc - 1)], send_row.at[it])
    for it in range(3):
        wait(col_y.at[it, pl.ds(1, NY - 1)], send_y.at[it])
        wait(col_z.at[it, pl.ds(1, nz - 1)], send_z.at[it])
    wait(sib_out, send_sib)
    wait(pair, send_x)


def solution(mesh):
    nz = mesh.shape["rows"] // NY
    nc = mesh.shape["cols"]

    def shards(noise, data):
        data = data.T
        rows, feats = noise.shape
        depth, dcols = data.shape
        dma = pltpu.SemaphoreType.DMA
        vmem = pl.BlockSpec(memory_space=pltpu.VMEM)

        def body(*refs):
            kernel(nz, *refs)

        return pl.pallas_call(
            body,
            out_shape=jax.ShapeDtypeStruct((rows, feats), BF16),
            in_specs=[pl.BlockSpec(memory_space=pl.ANY)] * 2,
            out_specs=vmem,
            scratch_shapes=[
                pltpu.VMEM((FEATURES, dcols), BF16),
                pltpu.VMEM((nc, rows, feats), BF16),
                pltpu.VMEM((rows, dcols), F32),
                pltpu.VMEM((1, dcols), F32),
                pltpu.VMEM((4, nc, 1, rows), F32),
                pltpu.VMEM((3, NY, 1, dcols), F32),
                pltpu.VMEM((3, nz, 1, dcols), F32),
                pltpu.VMEM((NX, rows, feats), BF16),
                pltpu.VMEM((NX, rows, feats), BF16),
                pltpu.VMEM((6, rows, feats // 2), BF16),
                pltpu.VMEM((2, rows, feats // 2), BF16),
                pltpu.VMEM((4, rows, feats // 2), BF16),
                pltpu.VMEM((rows, feats), F32),
                dma((2,)), dma((nz * NY,)), dma((nz * NY * 2,)), dma((nz * 2,)), dma((nc,)),
                dma((4,)), dma((3,)), dma((3,)), dma((NX,)), dma((2,)), dma((4,)),
                dma, dma, dma, dma, dma, dma, dma((4,)), dma((3,)), dma((3,)), dma, dma,
            ],
            compiler_params=pltpu.CompilerParams(
                collective_id=0, has_side_effects=True, vmem_limit_bytes=40 * 2**20
            ),
        )(noise, data)

    return jax.shard_map(
        shards,
        mesh=mesh,
        in_specs=(P("rows", "cols"), P("cols", "rows")),
        out_specs=P("rows", "cols"),
        check_vma=False,
    )
```

```python
import math

import jax
import jax.numpy as jnp
from jax import lax
from jax.experimental import pallas as pl
from jax.experimental.pallas import tpu as pltpu
from jax.sharding import PartitionSpec as P

FEATURES = 4096
NY = 4
NX = 4
F32 = jnp.float32
BF16 = jnp.bfloat16
NT = (((1,), (1,)), ((), ()))
FAR = 3
PART_A = 16


def kernel(
    nz, noise_ref, data_ref, out_ref,
    gathered, noise_all, dist, square, row_box, col_y, col_near, col_far, sib_out, sib_in, pair, relay, inbox, own,
    local, recv_a, recv_b, recv_q, recv_n, recv_row, recv_y, recv_near, recv_far, recv_sib, recv_relay, recv_in,
    send_a, send_b, send_ya, send_yb, send_q, send_n, send_row, send_y, send_near, send_far, send_sib, send_x,
):
    nc = 2 * NX
    rows, feats = noise_ref.shape
    depth, dcols = data_ref.shape
    part_b = depth - PART_A
    half = dcols // 2
    fhalf = feats // 2
    log_noise = math.log(rows * nz * NY)
    log_data = math.log(dcols * nc)

    me_r, me_c = lax.axis_index("rows"), lax.axis_index("cols")
    z, y = me_r // NY, lax.rem(me_r, NY)
    x, core = me_c // 2, lax.rem(me_c, 2)

    def at_z(k):
        return (lax.rem(z + k + nz, nz) * NY + y, me_c)

    def at_y(k):
        return (z * NY + lax.rem(y + k + NY, NY), me_c)

    def at_c(k):
        return (me_r, lax.rem(me_c + k + nc, nc))

    def at_x(k):
        return (me_r, lax.rem(x + k + NX, NX) * 2 + core)

    sibling = (me_r, x * 2 + 1 - core)

    def send(src, dst, send_sem, recv_sem, device):
        pltpu.make_async_remote_copy(
            src_ref=src, dst_ref=dst, send_sem=send_sem, recv_sem=recv_sem,
            device_id=device, device_id_type=pl.DeviceIdType.MESH,
        ).start()

    def wait(ref, sem):
        pltpu.make_async_copy(ref, ref, sem).wait()

    barrier = pltpu.get_barrier_semaphore()
    partners = [at_z(1), at_z(-1), sibling] + [at_y(k) for k in range(1, NY)] + [at_x(k) for k in range(1, NX)]
    for device in partners:
        pl.semaphore_signal(barrier, inc=1, device_id=device, device_id_type=pl.DeviceIdType.MESH)

    def chunk_a(chunk):
        return gathered.at[pl.ds(pl.multiple_of(chunk * depth, 16), PART_A)]

    def chunk_b(chunk, p):
        return gathered.at[pl.ds(pl.multiple_of(chunk * depth + PART_A, 16), part_b), p * half:(p + 1) * half]

    keep_data = pltpu.make_async_copy(
        data_ref, gathered.at[pl.ds(pl.multiple_of(me_r * depth, 16), depth)], local.at[0])
    keep_noise = pltpu.make_async_copy(noise_ref, noise_all.at[me_c], local.at[1])
    keep_data.start()
    keep_noise.start()
    pl.semaphore_wait(barrier, len(partners))

    my_a = data_ref.at[pl.ds(0, PART_A)]
    a = chunk_a(me_r)
    for p in (0, 1):
        my_b = data_ref.at[pl.ds(PART_A, part_b), p * half:(p + 1) * half]
        for d in (1, -1):
            send(my_b, chunk_b(me_r, p), send_b, recv_b.at[me_r * 2 + p], at_z(d))
    for k in (1, 3, 2):
        send(my_a, a, send_ya, recv_a.at[me_r], at_y(k))
    for d in (1, -1):
        send(my_a, a, send_a, recv_a.at[me_r], at_z(d))
    for p in (0, 1):
        my_b = data_ref.at[pl.ds(PART_A, part_b), p * half:(p + 1) * half]
        for d in (1, -1):
            send(my_b, chunk_b(me_r, p), send_yb, recv_b.at[me_r * 2 + p], at_y(d))

    mine = noise_all.at[me_c]
    for k in (1, 3, 2):
        send(noise_ref, mine, send_n, recv_n.at[me_c], at_x(k))
    send(noise_ref, mine, send_n, recv_n.at[me_c], sibling)

    def plane(step):
        return lax.rem(z + step + nz, nz)

    def part_a(step, k, ways):
        chunk = plane(-step) * NY + lax.rem(y + k, NY)
        ref = chunk_a(chunk)
        wait(ref, recv_a.at[chunk])
        for d in ways:
            send(ref, ref, send_a, recv_a.at[chunk], at_z(d))

    def part_b_z(p, step, ways, opposite=False):
        chunk = plane(-step) * NY + y
        ref, sem = chunk_b(chunk, p), recv_b.at[chunk * 2 + p]
        wait(ref, sem)
        for d in ways:
            send(ref, ref, send_b, sem, at_z(d))
        for d in (1, -1):
            send(ref, ref, send_yb, sem, at_y(d))
        if opposite:
            send(ref, ref, send_q, recv_q.at[plane(-step) * 2 + p], at_y(2))

    def part_b_y(p, step):
        d = 1 - 2 * p
        z0 = plane(-step)
        chunk = z0 * NY + lax.rem(y - d + NY, NY)
        ref = chunk_b(chunk, p)
        wait(ref, recv_b.at[chunk * 2 + p])
        send(ref, ref, send_q, recv_q.at[z0 * 2 + p], at_y(d))

    def gather_step(ends, befores, opposite=False):
        for p in (0, 1):
            for s, ways in ends:
                part_b_z(p, s, ways, opposite)
            for s, ways in befores:
                part_b_y(p, s)
        for k in (3, 1):
            for s, ways in befores:
                part_a(s, k, ways)
        for s, ways in ends:
            part_a(s, 0, ways)
        for s, ways in befores:
            part_a(s, 2, ways)

    last = nz // 2
    both = (1, -1)

    def inner_step(step, carry):
        gather_step(((step, (1,)), (-step, (-1,))), ((step - 1, (1,)), (1 - step, (-1,))))
        return carry

    for p in (0, 1):
        for d in both:
            part_b_z(p, d, (d,))
    for k in (3, 1):
        part_a(0, k, both)
    for p in (0, 1):
        part_b_y(p, 0)
    for d in both:
        part_a(d, 0, (d,))
    part_a(0, 2, both)
    lax.fori_loop(2, last - 3, inner_step, 0)
    for k in (1, 3, 2):
        c = lax.rem(x + k, NX) * 2 + core
        ref = noise_all.at[c]
        wait(ref, recv_n.at[c])
        send(ref, ref, send_n, recv_n.at[c], sibling)
    inner_step(last - 3, 0)
    for k in range(NX):
        c = lax.rem(x + k, NX) * 2 + 1 - core
        wait(noise_all.at[c], recv_n.at[c])
    keep_data.wait()
    keep_noise.wait()

    width = NY * depth

    def noise_step(c, total):
        n = noise_all[c].astype(F32)
        return total + jnp.sum(n * n, axis=1, keepdims=True)

    noise_sq = lax.fori_loop(0, nc, noise_step, jnp.zeros((rows, 1), F32))
    square[...] = jnp.zeros_like(square)
    dist[...] = jnp.zeros_like(dist)

    def arrived(z0):
        left, right, across = (z0 * NY + lax.rem(y + k, NY) for k in (3, 1, 2))
        wait(chunk_b(left, 1), recv_b.at[left * 2 + 1])
        wait(chunk_b(right, 0), recv_b.at[right * 2])
        for p in (0, 1):
            wait(chunk_b(across, p), recv_q.at[z0 * 2 + p])

    def product(step):
        z0 = plane(step)
        arrived(z0)
        d = gathered[pl.ds(pl.multiple_of(z0 * width, 16), width), :]
        first = pl.multiple_of(lax.rem(z0, feats // width) * width, width)
        n = noise_all[z0 // (feats // width), :, pl.ds(first, width)]
        dist[...] += jnp.dot(n, d, preferred_element_type=F32)
        d = d.astype(F32)
        square[...] += jnp.sum(d * d, axis=0, keepdims=True)

    def products(first, stop):
        def step(i, carry):
            product(first + i)
            return carry

        lax.fori_loop(0, stop - first, step, 0)

    products(-1, 2)
    inner_step(last - 2, 0)
    products(-3, -1)
    products(2, 4)
    s = last - 1
    gather_step(((s, (1,)), (-s, ())), ((s - 1, (1,)), (1 - s, (-1,))))
    products(1 - s + 1, -3)
    products(4, s - 1)
    gather_step(((last, ()),), ((s, (1,)), (-s, ())), opposite=True)
    products(1 - s, 2 - s)
    products(s - 1, s)
    for k, p in ((3, 0), (1, 1)):
        chunk = plane(-last) * NY + lax.rem(y + k, NY)
        wait(chunk_b(chunk, p), recv_b.at[chunk * 2 + p])
    for k in (3, 1, 2):
        part_a(last, k, ())
    products(-s, 1 - s)
    products(s, last + 1)
    dist[...] = (noise_sq + square[...] - 2.0 * dist[...]) / math.sqrt(FEATURES)

    def to_lanes(column):
        return jnp.transpose(jnp.broadcast_to(column, (rows, 128)))[0:1, :]

    def to_column(lanes):
        return jnp.transpose(jnp.broadcast_to(lanes, (128, rows)))[:, 0:1]

    def logsum(*parts):
        top = jnp.max(parts[0], axis=0)
        for part in parts[1:]:
            top = jnp.maximum(top, jnp.max(part, axis=0))
        return top + jnp.log(sum(jnp.sum(jnp.exp(part - top), axis=0) for part in parts))

    def plainsum(*parts):
        return sum(jnp.sum(part, axis=0) for part in parts)

    def over_cols(it, value):
        row_box[it, 0] = value
        for k in range(1, nc):
            send(row_box.at[it, 0], row_box.at[it, nc - k], send_row.at[it], recv_row.at[it], at_c(k))
        wait(row_box.at[it, pl.ds(1, nc - 1)], recv_row.at[it])
        return row_box[it]

    near = [d * k for k in range(last - FAR, 0, -1) for d in (1, -1)]
    far = [last] + [d * k for k in range(last - 1, last - FAR, -1) for d in (1, -1)]

    def over_rows(it, value, combine):
        col_y[it, 0] = value
        mine = col_y.at[it, 0]
        for k in (2, 1, 3):
            send(mine, col_y.at[it, NY - k], send_y.at[it], recv_y.at[it], at_y(k))
        for d in far:
            for k in (2, 1, 3, 0):
                slot = far.index(d if d == last else -d) * NY + (-k) % NY
                place = (lax.rem(z + d + nz, nz) * NY + lax.rem(y + k, NY), me_c)
                send(mine, col_far.at[it, slot], send_far.at[it], recv_far.at[it], place)
        wait(col_y.at[it, pl.ds(1, NY - 1)], recv_y.at[it])
        col_near[it, 0] = combine(col_y[it])
        for d in near:
            send(col_near.at[it, 0], col_near.at[it, 1 + near.index(-d)], send_near.at[it], recv_near.at[it], at_z(d))
        wait(col_far.at[it], recv_far.at[it])
        wait(col_near.at[it, pl.ds(1, len(near))], recv_near.at[it])
        return combine(col_near[it], col_far[it])

    scores = -dist[...]
    top = jnp.max(scores, axis=1, keepdims=True)
    logs = top + jnp.log(jnp.sum(jnp.exp(scores - top), axis=1, keepdims=True))
    u = to_column(-log_noise - logsum(over_cols(0, to_lanes(logs))))

    scores = u - dist[...]
    top = jnp.max(scores, axis=0, keepdims=True)
    logs = top + jnp.log(jnp.sum(jnp.exp(scores - top), axis=0, keepdims=True))
    v = -log_data - over_rows(0, logs, logsum)

    for it in (1, 2):
        total = jnp.sum(jnp.exp(u + v - dist[...]), axis=1, keepdims=True)
        total = plainsum(over_cols(it, to_lanes(total)))
        u = u - to_column(log_noise + jnp.log(total))
        total = jnp.sum(jnp.exp(u + v - dist[...]), axis=0, keepdims=True)
        v = v - (log_data + jnp.log(over_rows(it, total, plainsum)))

    weights = jnp.exp(u + v - dist[...] + log_noise)
    coupling = weights.astype(BF16)

    def share(c):
        d = gathered[pl.ds(pl.multiple_of(c * feats, 16), feats), :]
        return lax.dot_general(coupling, d, NT, preferred_element_type=F32)

    def other(k):
        sib_out[k] = share(lax.rem(x + k, NX) * 2 + 1 - core).astype(BF16)
        send(sib_out.at[k], sib_in.at[k], send_sib, recv_sib.at[k], sibling)

    def both(k):
        block = share(lax.rem(x + k, NX) * 2 + core)
        wait(sib_in.at[k], recv_sib.at[k])
        return block + sib_in[k].astype(F32)

    other(2)
    other(1)
    block = both(2)
    pair[2] = block[:, :fhalf].astype(BF16)
    pair[5] = block[:, fhalf:].astype(BF16)
    send(pair.at[2], relay.at[0], send_x, recv_relay.at[0], at_x(1))
    send(pair.at[5], relay.at[1], send_x, recv_relay.at[1], at_x(-1))
    other(3)
    right = both(1)
    pair[1] = right[:, fhalf:].astype(BF16)
    send(pair.at[1], inbox.at[1], send_x, recv_in.at[1], at_x(1))
    left = both(3)
    pair[3] = left[:, :fhalf].astype(BF16)
    send(pair.at[3], inbox.at[2], send_x, recv_in.at[2], at_x(-1))
    row_box[3, 0] = to_lanes(jnp.sum(weights, axis=1, keepdims=True))
    for k in range(1, nc):
        send(row_box.at[3, 0], row_box.at[3, nc - k], send_row.at[3], recv_row.at[3], at_c(k))
    other(0)
    wait(relay.at[0], recv_relay.at[0])
    pair[0] = (right[:, :fhalf] + relay[0].astype(F32)).astype(BF16)
    send(pair.at[0], inbox.at[0], send_x, recv_in.at[0], at_x(1))
    wait(relay.at[1], recv_relay.at[1])
    pair[4] = (left[:, fhalf:] + relay[1].astype(F32)).astype(BF16)
    send(pair.at[4], inbox.at[3], send_x, recv_in.at[3], at_x(-1))
    own[...] = both(0)
    wait(row_box.at[3, pl.ds(1, nc - 1)], recv_row.at[3])
    scale = to_column(1.0 / jnp.sum(row_box[3], axis=0))
    for i in (1, 2, 0, 3):
        wait(inbox.at[i], recv_in.at[i])
    low = own[:, :fhalf] + inbox[0].astype(F32) + inbox[2].astype(F32)
    high = own[:, fhalf:] + inbox[1].astype(F32) + inbox[3].astype(F32)
    out_ref[:, :fhalf] = (low * scale).astype(BF16)
    out_ref[:, fhalf:] = (high * scale).astype(BF16)

    hops = nz - 1
    wait(gathered.at[pl.ds(0, hops * NY * PART_A)], send_a)
    wait(gathered.at[pl.ds(0, hops * part_b)], send_b)
    wait(gathered.at[pl.ds(0, 3 * PART_A)], send_ya)
    wait(gathered.at[pl.ds(0, 2 * nz * part_b)], send_yb)
    wait(gathered.at[pl.ds(0, nz * part_b)], send_q)
    wait(noise_all.at[pl.ds(0, nc - 1)], send_n)
    for it in range(4):
        wait(row_box.at[it, pl.ds(1, nc - 1)], send_row.at[it])
    for it in range(3):
        wait(col_y.at[it, pl.ds(1, NY - 1)], send_y.at[it])
        wait(col_far.at[it], send_far.at[it])
        wait(col_near.at[it, pl.ds(1, len(near))], send_near.at[it])
    wait(sib_out, send_sib)
    wait(pair, send_x)


def solution(mesh):
    nz = mesh.shape["rows"] // NY
    nc = mesh.shape["cols"]

    def shards(noise, data):
        data = data.T
        rows, feats = noise.shape
        depth, dcols = data.shape
        dma = pltpu.SemaphoreType.DMA
        vmem = pl.BlockSpec(memory_space=pltpu.VMEM)

        def body(*refs):
            kernel(nz, *refs)

        return pl.pallas_call(
            body,
            out_shape=jax.ShapeDtypeStruct((rows, feats), BF16),
            in_specs=[pl.BlockSpec(memory_space=pl.ANY)] * 2,
            out_specs=vmem,
            scratch_shapes=[
                pltpu.VMEM((FEATURES, dcols), BF16),
                pltpu.VMEM((nc, rows, feats), BF16),
                pltpu.VMEM((rows, dcols), F32),
                pltpu.VMEM((1, dcols), F32),
                pltpu.VMEM((4, nc, 1, rows), F32),
                pltpu.VMEM((3, NY, 1, dcols), F32),
                pltpu.VMEM((3, nz - 2 * FAR + 1, 1, dcols), F32),
                pltpu.VMEM((3, (2 * FAR - 1) * NY, 1, dcols), F32),
                pltpu.VMEM((NX, rows, feats), BF16),
                pltpu.VMEM((NX, rows, feats), BF16),
                pltpu.VMEM((6, rows, feats // 2), BF16),
                pltpu.VMEM((2, rows, feats // 2), BF16),
                pltpu.VMEM((4, rows, feats // 2), BF16),
                pltpu.VMEM((rows, feats), F32),
                dma((2,)), dma((nz * NY,)), dma((nz * NY * 2,)), dma((nz * 2,)), dma((nc,)),
                dma((4,)), dma((3,)), dma((3,)), dma((3,)), dma((NX,)), dma((2,)), dma((4,)),
                dma, dma, dma, dma, dma, dma, dma((4,)), dma((3,)), dma((3,)), dma((3,)), dma, dma,
            ],
            compiler_params=pltpu.CompilerParams(
                collective_id=0, has_side_effects=True, vmem_limit_bytes=40 * 2**20
            ),
        )(noise, data)

    return jax.shard_map(
        shards,
        mesh=mesh,
        in_specs=(P("rows", "cols"), P("cols", "rows")),
        out_specs=P("rows", "cols"),
        check_vma=False,
    )
```

```python
import math

import jax
import jax.numpy as jnp
from jax import lax
from jax.experimental import pallas as pl
from jax.experimental.pallas import tpu as pltpu
from jax.sharding import PartitionSpec as P

FEATURES = 4096
NY = 4
NX = 4
F32 = jnp.float32
BF16 = jnp.bfloat16
NT = (((1,), (1,)), ((), ()))
FAR = 3
PART_A = 16


def kernel(
    nz, noise_ref, data_ref, out_ref,
    gathered, noise_all, dist, square, noise_square, row_box, col_y, col_near, col_far, sib_out, sib_in, pair, relay, inbox, own,
    local, recv_a, recv_b, recv_q, recv_n, recv_row, recv_y, recv_near, recv_far, recv_sib, recv_relay, recv_in,
    send_a, send_b, send_ya, send_yb, send_q, send_n, send_row, send_y, send_near, send_far, send_sib, send_x,
):
    nc = 2 * NX
    rows, feats = noise_ref.shape
    depth, dcols = data_ref.shape
    part_b = depth - PART_A
    half = dcols // 2
    fhalf = feats // 2
    log_noise = math.log(rows * nz * NY)
    log_data = math.log(dcols * nc)

    me_r, me_c = lax.axis_index("rows"), lax.axis_index("cols")
    z, y = me_r // NY, lax.rem(me_r, NY)
    x, core = me_c // 2, lax.rem(me_c, 2)

    def at_z(k):
        return (lax.rem(z + k + nz, nz) * NY + y, me_c)

    def at_y(k):
        return (z * NY + lax.rem(y + k + NY, NY), me_c)

    def at_c(k):
        return (me_r, lax.rem(me_c + k + nc, nc))

    def at_x(k):
        return (me_r, lax.rem(x + k + NX, NX) * 2 + core)

    sibling = (me_r, x * 2 + 1 - core)

    def send(src, dst, send_sem, recv_sem, device):
        pltpu.make_async_remote_copy(
            src_ref=src, dst_ref=dst, send_sem=send_sem, recv_sem=recv_sem,
            device_id=device, device_id_type=pl.DeviceIdType.MESH,
        ).start()

    def wait(ref, sem):
        pltpu.make_async_copy(ref, ref, sem).wait()

    barrier = pltpu.get_barrier_semaphore()
    partners = [at_z(1), at_z(-1), sibling] + [at_y(k) for k in range(1, NY)] + [at_x(k) for k in range(1, NX)]
    for device in partners:
        pl.semaphore_signal(barrier, inc=1, device_id=device, device_id_type=pl.DeviceIdType.MESH)

    def chunk_a(chunk):
        return gathered.at[pl.ds(pl.multiple_of(chunk * depth, 16), PART_A)]

    def chunk_b(chunk, p):
        return gathered.at[pl.ds(pl.multiple_of(chunk * depth + PART_A, 16), part_b), p * half:(p + 1) * half]

    keep_data = pltpu.make_async_copy(
        data_ref, gathered.at[pl.ds(pl.multiple_of(me_r * depth, 16), depth)], local.at[0])
    keep_noise = pltpu.make_async_copy(noise_ref, noise_all.at[me_c], local.at[1])
    keep_data.start()
    keep_noise.start()
    pl.semaphore_wait(barrier, len(partners))

    my_a = data_ref.at[pl.ds(0, PART_A)]
    a = chunk_a(me_r)
    for p in (0, 1):
        my_b = data_ref.at[pl.ds(PART_A, part_b), p * half:(p + 1) * half]
        for d in (1, -1):
            send(my_b, chunk_b(me_r, p), send_b, recv_b.at[me_r * 2 + p], at_z(d))
    for k in (1, 3, 2):
        send(my_a, a, send_ya, recv_a.at[me_r], at_y(k))
    for d in (1, -1):
        send(my_a, a, send_a, recv_a.at[me_r], at_z(d))
    for p in (0, 1):
        my_b = data_ref.at[pl.ds(PART_A, part_b), p * half:(p + 1) * half]
        for d in (1, -1):
            send(my_b, chunk_b(me_r, p), send_yb, recv_b.at[me_r * 2 + p], at_y(d))

    mine = noise_all.at[me_c]
    for k in (1, 3, 2):
        send(noise_ref, mine, send_n, recv_n.at[me_c], at_x(k))
    send(noise_ref, mine, send_n, recv_n.at[me_c], sibling)

    def plane(step):
        return lax.rem(z + step + nz, nz)

    def part_a(step, k, ways):
        chunk = plane(-step) * NY + lax.rem(y + k, NY)
        ref = chunk_a(chunk)
        wait(ref, recv_a.at[chunk])
        for d in ways:
            send(ref, ref, send_a, recv_a.at[chunk], at_z(d))

    def part_b_z(p, step, ways, opposite=False):
        chunk = plane(-step) * NY + y
        ref, sem = chunk_b(chunk, p), recv_b.at[chunk * 2 + p]
        wait(ref, sem)
        for d in ways:
            send(ref, ref, send_b, sem, at_z(d))
        for d in (1, -1):
            send(ref, ref, send_yb, sem, at_y(d))
        if opposite:
            send(ref, ref, send_q, recv_q.at[plane(-step) * 2 + p], at_y(2))

    def part_b_y(p, step):
        d = 1 - 2 * p
        z0 = plane(-step)
        chunk = z0 * NY + lax.rem(y - d + NY, NY)
        ref = chunk_b(chunk, p)
        wait(ref, recv_b.at[chunk * 2 + p])
        send(ref, ref, send_q, recv_q.at[z0 * 2 + p], at_y(d))

    def gather_step(ends, befores, opposite=False):
        for p in (0, 1):
            for s, ways in ends:
                part_b_z(p, s, ways, opposite)
            for s, ways in befores:
                part_b_y(p, s)
        for k in (3, 1):
            for s, ways in befores:
                part_a(s, k, ways)
        for s, ways in ends:
            part_a(s, 0, ways)
        for s, ways in befores:
            part_a(s, 2, ways)

    last = nz // 2
    both = (1, -1)

    def inner_step(step, carry):
        gather_step(((step, (1,)), (-step, (-1,))), ((step - 1, (1,)), (1 - step, (-1,))))
        return carry

    for p in (0, 1):
        for d in both:
            part_b_z(p, d, (d,))
    for k in (3, 1):
        part_a(0, k, both)
    for p in (0, 1):
        part_b_y(p, 0)
    for d in both:
        part_a(d, 0, (d,))
    part_a(0, 2, both)
    lax.fori_loop(2, last - 3, inner_step, 0)
    for k in (1, 3, 2):
        c = lax.rem(x + k, NX) * 2 + core
        ref = noise_all.at[c]
        wait(ref, recv_n.at[c])
        send(ref, ref, send_n, recv_n.at[c], sibling)
    inner_step(last - 3, 0)
    for k in range(NX):
        c = lax.rem(x + k, NX) * 2 + 1 - core
        wait(noise_all.at[c], recv_n.at[c])
    keep_data.wait()
    keep_noise.wait()

    width = NY * depth

    def tiles(width):
        return [slice(i, i + 128) for i in range(0, width, 128)]

    def noise_squares(first, stop):
        def step(i, carry):
            total = noise_square[...]
            for t in tiles(feats):
                n = noise_all[first + i, :, t].astype(F32)
                total += n * n
            noise_square[...] = total
            return carry

        lax.fori_loop(0, stop - first, step, 0)

    noise_square[...] = jnp.zeros_like(noise_square)
    square[...] = jnp.zeros_like(square)
    dist[...] = jnp.zeros_like(dist)

    def arrived(z0):
        left, right, across = (z0 * NY + lax.rem(y + k, NY) for k in (3, 1, 2))
        wait(chunk_b(left, 1), recv_b.at[left * 2 + 1])
        wait(chunk_b(right, 0), recv_b.at[right * 2])
        for p in (0, 1):
            wait(chunk_b(across, p), recv_q.at[z0 * 2 + p])

    def product(step):
        z0 = plane(step)
        arrived(z0)
        d = gathered[pl.ds(pl.multiple_of(z0 * width, 16), width), :]
        first = pl.multiple_of(lax.rem(z0, feats // width) * width, width)
        n = noise_all[z0 // (feats // width), :, pl.ds(first, width)]
        dist[...] += jnp.dot(n, d, preferred_element_type=F32)
        d = d.astype(F32)
        square[...] += jnp.sum(d * d, axis=0, keepdims=True)

    def products(first, stop):
        def step(i, carry):
            product(first + i)
            return carry

        lax.fori_loop(0, stop - first, step, 0)

    noise_squares(0, nc // 2)
    product(0)
    inner_step(last - 2, 0)
    noise_squares(nc // 2, nc)
    products(-1, 0)
    products(1, 2)
    s = last - 1
    gather_step(((s, (1,)), (-s, ())), ((s - 1, (1,)), (1 - s, (-1,))))
    products(-3, -1)
    products(2, 4)
    gather_step(((last, ()),), ((s, (1,)), (-s, ())), opposite=True)
    products(1 - s, -3)
    products(4, s)
    for k, p in ((3, 0), (1, 1)):
        chunk = plane(-last) * NY + lax.rem(y + k, NY)
        wait(chunk_b(chunk, p), recv_b.at[chunk * 2 + p])
    for k in (3, 1, 2):
        part_a(last, k, ())
    products(-s, 1 - s)
    products(s, last + 1)
    noise_sq = jnp.sum(noise_square[...], axis=1, keepdims=True)
    dist[...] = (noise_sq + square[...] - 2.0 * dist[...]) / math.sqrt(FEATURES)

    def gather_left():
        hops = nz - 1
        wait(gathered.at[pl.ds(0, hops * NY * PART_A)], send_a)
        wait(gathered.at[pl.ds(0, hops * part_b)], send_b)
        wait(gathered.at[pl.ds(0, 3 * PART_A)], send_ya)
        wait(gathered.at[pl.ds(0, 2 * nz * part_b)], send_yb)
        wait(gathered.at[pl.ds(0, nz * part_b)], send_q)
        wait(noise_all.at[pl.ds(0, nc - 1)], send_n)

    def row_left(it):
        wait(row_box.at[it, pl.ds(1, nc - 1)], send_row.at[it])

    def col_left(it):
        wait(col_y.at[it, pl.ds(1, NY - 1)], send_y.at[it])
        wait(col_far.at[it], send_far.at[it])
        wait(col_near.at[it, pl.ds(1, len(near))], send_near.at[it])

    def sum_lanes(block):
        return jnp.sum(jnp.transpose(block), axis=0, keepdims=True)

    def to_column(lanes):
        return jnp.transpose(jnp.broadcast_to(lanes, (128, rows)))

    def logsum(*parts):
        top = jnp.max(parts[0], axis=0)
        for part in parts[1:]:
            top = jnp.maximum(top, jnp.max(part, axis=0))
        return top + jnp.log(sum(jnp.sum(jnp.exp(part - top), axis=0) for part in parts))

    def plainsum(*parts):
        return sum(jnp.sum(part, axis=0) for part in parts)

    def over_cols(it, value):
        row_box[it, 0] = value
        for k in sorted(range(1, nc), key=lambda k: abs(k - NX)):
            send(row_box.at[it, 0], row_box.at[it, nc - k], send_row.at[it], recv_row.at[it], at_c(k))
        if it == 0:
            gather_left()
        else:
            row_left(it - 1)
            col_left(it - 1)
        wait(row_box.at[it, pl.ds(1, nc - 1)], recv_row.at[it])
        return row_box[it]

    near = [d * k for k in range(last - FAR, 0, -1) for d in (1, -1)]
    far = [last] + [d * k for k in range(last - 1, last - FAR, -1) for d in (1, -1)]

    def over_rows(it, value, combine):
        col_y[it, 0] = value
        mine = col_y.at[it, 0]
        for k in (2, 1, 3):
            send(mine, col_y.at[it, NY - k], send_y.at[it], recv_y.at[it], at_y(k))
        for d in far:
            for k in (2, 1, 3, 0):
                slot = far.index(d if d == last else -d) * NY + (-k) % NY
                place = (lax.rem(z + d + nz, nz) * NY + lax.rem(y + k, NY), me_c)
                send(mine, col_far.at[it, slot], send_far.at[it], recv_far.at[it], place)
        wait(col_y.at[it, pl.ds(1, NY - 1)], recv_y.at[it])
        col_near[it, 0] = combine(col_y[it])
        for d in near:
            send(col_near.at[it, 0], col_near.at[it, 1 + near.index(-d)], send_near.at[it], recv_near.at[it], at_z(d))
        wait(col_far.at[it], recv_far.at[it])
        wait(col_near.at[it, pl.ds(1, len(near))], recv_near.at[it])
        return combine(col_near[it], col_far[it])

    scores = [-dist[:, t] for t in tiles(dcols)]
    top = jnp.max(jnp.maximum(jnp.maximum(scores[0], scores[1]), jnp.maximum(scores[2], scores[3])), axis=1, keepdims=True)
    logs = top + jnp.log(jnp.sum(sum(jnp.exp(score - top) for score in scores), axis=1, keepdims=True))
    logs = jnp.transpose(jnp.broadcast_to(logs, (rows, 128)))[0:1, :]
    u = to_column(-log_noise - logsum(over_cols(0, logs)))

    logs = []
    for t in tiles(dcols):
        scores = u - dist[:, t]
        top = jnp.max(scores, axis=0, keepdims=True)
        logs.append(top + jnp.log(jnp.sum(jnp.exp(scores - top), axis=0, keepdims=True)))
    v = -log_data - over_rows(0, jnp.concatenate(logs, axis=1), logsum)

    def shifted(u, v):
        return [jnp.exp(u + v[:, t] - dist[:, t]) for t in tiles(dcols)]

    for it in (1, 2):
        total = plainsum(over_cols(it, sum_lanes(sum(shifted(u, v)))))
        u = u - to_column(log_noise + jnp.log(total))
        total = jnp.concatenate([jnp.sum(part, axis=0, keepdims=True) for part in shifted(u, v)], axis=1)
        v = v - (log_data + jnp.log(over_rows(it, total, plainsum)))

    total = jnp.zeros((rows, 128), F32)
    for t in tiles(dcols):
        part = jnp.exp(u + v[:, t] - dist[:, t] + log_noise)
        total += part
        out_ref[:, t] = part.astype(BF16)

    def share(c):
        d = gathered[pl.ds(pl.multiple_of(c * feats, 16), feats), :]
        return lax.dot_general(out_ref[...], d, NT, preferred_element_type=F32)

    def other(k):
        sib_out[k] = share(lax.rem(x + k, NX) * 2 + 1 - core).astype(BF16)
        send(sib_out.at[k], sib_in.at[k], send_sib, recv_sib.at[k], sibling)

    def both(k):
        block = share(lax.rem(x + k, NX) * 2 + core)
        wait(sib_in.at[k], recv_sib.at[k])
        return block + sib_in[k].astype(F32)

    other(2)
    other(1)
    block = both(2)
    pair[2] = block[:, :fhalf].astype(BF16)
    pair[5] = block[:, fhalf:].astype(BF16)
    send(pair.at[2], relay.at[0], send_x, recv_relay.at[0], at_x(1))
    send(pair.at[5], relay.at[1], send_x, recv_relay.at[1], at_x(-1))
    other(3)
    right = both(1)
    pair[1] = right[:, fhalf:].astype(BF16)
    send(pair.at[1], inbox.at[1], send_x, recv_in.at[1], at_x(1))
    left = both(3)
    pair[3] = left[:, :fhalf].astype(BF16)
    send(pair.at[3], inbox.at[2], send_x, recv_in.at[2], at_x(-1))
    row_box[3, 0] = sum_lanes(total)
    for k in range(1, nc):
        send(row_box.at[3, 0], row_box.at[3, nc - k], send_row.at[3], recv_row.at[3], at_c(k))
    other(0)
    wait(relay.at[0], recv_relay.at[0])
    pair[0] = (right[:, :fhalf] + relay[0].astype(F32)).astype(BF16)
    send(pair.at[0], inbox.at[0], send_x, recv_in.at[0], at_x(1))
    wait(relay.at[1], recv_relay.at[1])
    pair[4] = (left[:, fhalf:] + relay[1].astype(F32)).astype(BF16)
    send(pair.at[4], inbox.at[3], send_x, recv_in.at[3], at_x(-1))
    own[...] = both(0)
    row_left(2)
    col_left(2)
    wait(row_box.at[3, pl.ds(1, nc - 1)], recv_row.at[3])
    scale = to_column(1.0 / jnp.sum(row_box[3], axis=0))
    row_left(3)
    wait(sib_out, send_sib)
    for i in (1, 2, 0, 3):
        wait(inbox.at[i], recv_in.at[i])
    for first, i, k in ((0, 0, 2), (fhalf, 1, 3)):
        for t in tiles(fhalf):
            f = slice(first + t.start, first + t.stop)
            block = own[:, f] + inbox[i, :, t].astype(F32) + inbox[k, :, t].astype(F32)
            out_ref[:, f] = (block * scale).astype(BF16)
    wait(pair, send_x)


def solution(mesh):
    nz = mesh.shape["rows"] // NY
    nc = mesh.shape["cols"]

    def shards(noise, data):
        data = data.T
        rows, feats = noise.shape
        depth, dcols = data.shape
        dma = pltpu.SemaphoreType.DMA
        vmem = pl.BlockSpec(memory_space=pltpu.VMEM)

        def body(*refs):
            kernel(nz, *refs)

        return pl.pallas_call(
            body,
            out_shape=jax.ShapeDtypeStruct((rows, feats), BF16),
            in_specs=[pl.BlockSpec(memory_space=pl.ANY)] * 2,
            out_specs=vmem,
            scratch_shapes=[
                pltpu.VMEM((FEATURES, dcols), BF16),
                pltpu.VMEM((nc, rows, feats), BF16),
                pltpu.VMEM((rows, dcols), F32),
                pltpu.VMEM((1, dcols), F32),
                pltpu.VMEM((rows, 128), F32),
                pltpu.VMEM((4, nc, 1, rows), F32),
                pltpu.VMEM((3, NY, 1, dcols), F32),
                pltpu.VMEM((3, nz - 2 * FAR + 1, 1, dcols), F32),
                pltpu.VMEM((3, (2 * FAR - 1) * NY, 1, dcols), F32),
                pltpu.VMEM((NX, rows, feats), BF16),
                pltpu.VMEM((NX, rows, feats), BF16),
                pltpu.VMEM((6, rows, feats // 2), BF16),
                pltpu.VMEM((2, rows, feats // 2), BF16),
                pltpu.VMEM((4, rows, feats // 2), BF16),
                pltpu.VMEM((rows, feats), F32),
                dma((2,)), dma((nz * NY,)), dma((nz * NY * 2,)), dma((nz * 2,)), dma((nc,)),
                dma((4,)), dma((3,)), dma((3,)), dma((3,)), dma((NX,)), dma((2,)), dma((4,)),
                dma, dma, dma, dma, dma, dma, dma((4,)), dma((3,)), dma((3,)), dma((3,)), dma, dma,
            ],
            compiler_params=pltpu.CompilerParams(
                collective_id=0, has_side_effects=True, vmem_limit_bytes=54784 * 2**10
            ),
        )(noise, data)

    return jax.shard_map(
        shards,
        mesh=mesh,
        in_specs=(P("rows", "cols"), P("cols", "rows")),
        out_specs=P("rows", "cols"),
        check_vma=False,
    )
```

```python
import math

import jax
import jax.numpy as jnp
from jax import lax
from jax.experimental import pallas as pl
from jax.experimental.pallas import tpu as pltpu
from jax.sharding import PartitionSpec as P

FEATURES = 4096
NY = 4
NX = 4
F32 = jnp.float32
BF16 = jnp.bfloat16
NT = (((1,), (1,)), ((), ()))
FAR = 3
PART_A = 16


def kernel(
    nz, noise_ref, data_ref, out_ref,
    gathered, noise_all, dist, square, noise_square, row_box, col_y, col_near, col_far, sib_out, sib_in, pair, relay, inbox, own,
    local, recv_a, recv_b, recv_q, recv_n, recv_row, recv_y, recv_near, recv_far, recv_sib, recv_relay, recv_in,
    send_a, send_b, send_ya, send_yb, send_q, send_n, send_row, send_y, send_near, send_far, send_sib, send_x,
):
    nc = 2 * NX
    rows, feats = noise_ref.shape
    depth, dcols = data_ref.shape
    part_b = depth - PART_A
    half = dcols // 2
    fhalf = feats // 2
    log_noise = math.log(rows * nz * NY)
    log_data = math.log(dcols * nc)

    me_r, me_c = lax.axis_index("rows"), lax.axis_index("cols")
    z, y = me_r // NY, lax.rem(me_r, NY)
    x, core = me_c // 2, lax.rem(me_c, 2)

    def at_z(k):
        return (lax.rem(z + k + nz, nz) * NY + y, me_c)

    def at_y(k):
        return (z * NY + lax.rem(y + k + NY, NY), me_c)

    def at_c(k):
        return (me_r, lax.rem(me_c + k + nc, nc))

    def at_x(k):
        return (me_r, lax.rem(x + k + NX, NX) * 2 + core)

    sibling = (me_r, x * 2 + 1 - core)

    def send(src, dst, send_sem, recv_sem, device):
        pltpu.make_async_remote_copy(
            src_ref=src, dst_ref=dst, send_sem=send_sem, recv_sem=recv_sem,
            device_id=device, device_id_type=pl.DeviceIdType.MESH,
        ).start()

    def wait(ref, sem):
        pltpu.make_async_copy(ref, ref, sem).wait()

    barrier = pltpu.get_barrier_semaphore()
    partners = [at_z(1), at_z(-1), sibling] + [at_y(k) for k in range(1, NY)] + [at_x(k) for k in range(1, NX)]
    for device in partners:
        pl.semaphore_signal(barrier, inc=1, device_id=device, device_id_type=pl.DeviceIdType.MESH)

    def chunk_a(chunk):
        return gathered.at[pl.ds(pl.multiple_of(chunk * depth, 16), PART_A)]

    def chunk_b(chunk, p):
        return gathered.at[pl.ds(pl.multiple_of(chunk * depth + PART_A, 16), part_b), p * half:(p + 1) * half]

    keep_data = pltpu.make_async_copy(
        data_ref, gathered.at[pl.ds(pl.multiple_of(me_r * depth, 16), depth)], local.at[0])
    keep_noise = pltpu.make_async_copy(noise_ref, noise_all.at[me_c], local.at[1])
    keep_data.start()
    keep_noise.start()
    pl.semaphore_wait(barrier, len(partners))

    my_a = data_ref.at[pl.ds(0, PART_A)]
    a = chunk_a(me_r)
    for p in (0, 1):
        my_b = data_ref.at[pl.ds(PART_A, part_b), p * half:(p + 1) * half]
        for d in (1, -1):
            send(my_b, chunk_b(me_r, p), send_b, recv_b.at[me_r * 2 + p], at_z(d))
    for k in (1, 3, 2):
        send(my_a, a, send_ya, recv_a.at[me_r], at_y(k))
    for d in (1, -1):
        send(my_a, a, send_a, recv_a.at[me_r], at_z(d))
    for p in (0, 1):
        my_b = data_ref.at[pl.ds(PART_A, part_b), p * half:(p + 1) * half]
        for d in (1, -1):
            send(my_b, chunk_b(me_r, p), send_yb, recv_b.at[me_r * 2 + p], at_y(d))

    mine = noise_all.at[me_c]
    for k in (1, 3, 2):
        send(noise_ref, mine, send_n, recv_n.at[me_c], at_x(k))
    send(noise_ref, mine, send_n, recv_n.at[me_c], sibling)

    last = nz // 2

    def plane(step):
        return lax.rem(z + step + nz, nz)

    def part_a(step, k, ways):
        if isinstance(step, int) and last - 3 < step < last:
            ways = (1, 2) if step == last - 2 else ()
        chunk = plane(-step) * NY + lax.rem(y + k, NY)
        ref = chunk_a(chunk)
        wait(ref, recv_a.at[chunk])
        for d in ways:
            send(ref, ref, send_a, recv_a.at[chunk], at_z(d))

    def part_b_z(p, step, ways, opposite=False):
        chunk = plane(-step) * NY + y
        ref, sem = chunk_b(chunk, p), recv_b.at[chunk * 2 + p]
        wait(ref, sem)
        for d in ways:
            send(ref, ref, send_b, sem, at_z(d))
        for d in (1, -1):
            send(ref, ref, send_yb, sem, at_y(d))
        if opposite:
            send(ref, ref, send_q, recv_q.at[plane(-step) * 2 + p], at_y(2))

    def part_b_y(p, step):
        d = 1 - 2 * p
        z0 = plane(-step)
        chunk = z0 * NY + lax.rem(y - d + NY, NY)
        ref = chunk_b(chunk, p)
        wait(ref, recv_b.at[chunk * 2 + p])
        send(ref, ref, send_q, recv_q.at[z0 * 2 + p], at_y(d))

    def gather_step(ends, befores, opposite=False):
        for p in (0, 1):
            for s, ways in ends:
                part_b_z(p, s, ways, opposite)
            for s, ways in befores:
                part_b_y(p, s)
        for k in (3, 1):
            for s, ways in befores:
                part_a(s, k, ways)
        for s, ways in ends:
            part_a(s, 0, ways)
        for s, ways in befores:
            part_a(s, 2, ways)

    both = (1, -1)

    def inner_step(step, carry):
        gather_step(((step, (1,)), (-step, (-1,))), ((step - 1, (1,)), (1 - step, (-1,))))
        return carry

    for p in (0, 1):
        for d in both:
            part_b_z(p, d, (d,))
    for k in (3, 1):
        part_a(0, k, both)
    for p in (0, 1):
        part_b_y(p, 0)
    for d in both:
        part_a(d, 0, (d,))
    part_a(0, 2, both)
    lax.fori_loop(2, last - 3, inner_step, 0)
    for k in (1, 3, 2):
        c = lax.rem(x + k, NX) * 2 + core
        ref = noise_all.at[c]
        wait(ref, recv_n.at[c])
        send(ref, ref, send_n, recv_n.at[c], sibling)
    inner_step(last - 3, 0)
    for k in range(NX):
        c = lax.rem(x + k, NX) * 2 + 1 - core
        wait(noise_all.at[c], recv_n.at[c])
    keep_data.wait()
    keep_noise.wait()

    width = NY * depth

    def tiles(width):
        return [slice(i, i + 128) for i in range(0, width, 128)]

    def noise_squares(first, stop):
        def step(i, carry):
            total = noise_square[...]
            for t in tiles(feats):
                n = noise_all[first + i, :, t].astype(F32)
                total += n * n
            noise_square[...] = total
            return carry

        lax.fori_loop(0, stop - first, step, 0)

    noise_square[...] = jnp.zeros_like(noise_square)
    square[...] = jnp.zeros_like(square)
    dist[...] = jnp.zeros_like(dist)

    def arrived(z0):
        left, right, across = (z0 * NY + lax.rem(y + k, NY) for k in (3, 1, 2))
        wait(chunk_b(left, 1), recv_b.at[left * 2 + 1])
        wait(chunk_b(right, 0), recv_b.at[right * 2])
        for p in (0, 1):
            wait(chunk_b(across, p), recv_q.at[z0 * 2 + p])

    def product(step):
        z0 = plane(step)
        arrived(z0)
        d = gathered[pl.ds(pl.multiple_of(z0 * width, 16), width), :]
        first = pl.multiple_of(lax.rem(z0, feats // width) * width, width)
        n = noise_all[z0 // (feats // width), :, pl.ds(first, width)]
        dist[...] += jnp.dot(n, d, preferred_element_type=F32)
        d = d.astype(F32)
        square[...] += jnp.sum(d * d, axis=0, keepdims=True)

    def products(first, stop):
        def step(i, carry):
            product(first + i)
            return carry

        lax.fori_loop(0, stop - first, step, 0)

    noise_squares(0, nc // 2)
    product(0)
    inner_step(last - 2, 0)
    noise_squares(nc // 2, nc)
    products(-1, 0)
    products(1, 2)
    s = last - 1
    gather_step(((s, (1,)), (-s, ())), ((s - 1, (1,)), (1 - s, (-1,))))
    products(-3, -1)
    products(2, 4)
    gather_step(((last, ()),), ((s, (1,)), (-s, ())), opposite=True)
    products(1 - s, -3)
    products(4, s)
    for k, p in ((3, 0), (1, 1)):
        chunk = plane(-last) * NY + lax.rem(y + k, NY)
        wait(chunk_b(chunk, p), recv_b.at[chunk * 2 + p])
    for k in (3, 1, 2):
        part_a(last, k, ())
    products(-s, 1 - s)
    products(s, last + 1)
    noise_sq = jnp.sum(noise_square[...], axis=1, keepdims=True)
    dist[...] = (noise_sq + square[...] - 2.0 * dist[...]) / math.sqrt(FEATURES)

    def gather_left():
        hops = nz - 1
        wait(gathered.at[pl.ds(0, hops * NY * PART_A)], send_a)
        wait(gathered.at[pl.ds(0, hops * part_b)], send_b)
        wait(gathered.at[pl.ds(0, 3 * PART_A)], send_ya)
        wait(gathered.at[pl.ds(0, 2 * nz * part_b)], send_yb)
        wait(gathered.at[pl.ds(0, nz * part_b)], send_q)
        wait(noise_all.at[pl.ds(0, nc - 1)], send_n)

    def row_left(it):
        wait(row_box.at[it, pl.ds(1, nc - 1)], send_row.at[it])

    def col_left(it):
        wait(col_y.at[it, pl.ds(1, NY - 1)], send_y.at[it])
        wait(col_far.at[it], send_far.at[it])
        wait(col_near.at[it, pl.ds(1, len(near))], send_near.at[it])

    def sum_lanes(block):
        return jnp.sum(jnp.transpose(block), axis=0, keepdims=True)

    def to_column(lanes):
        return jnp.transpose(jnp.broadcast_to(lanes, (128, rows)))

    def logsum(*parts):
        top = jnp.max(parts[0], axis=0)
        for part in parts[1:]:
            top = jnp.maximum(top, jnp.max(part, axis=0))
        return top + jnp.log(sum(jnp.sum(jnp.exp(part - top), axis=0) for part in parts))

    def plainsum(*parts):
        return sum(jnp.sum(part, axis=0) for part in parts)

    def over_cols(it, value):
        row_box[it, 0] = value
        for k in sorted(range(1, nc), key=lambda k: abs(k - NX)):
            send(row_box.at[it, 0], row_box.at[it, nc - k], send_row.at[it], recv_row.at[it], at_c(k))
        if it == 0:
            gather_left()
        else:
            row_left(it - 1)
            col_left(it - 1)
        wait(row_box.at[it, pl.ds(1, nc - 1)], recv_row.at[it])
        return row_box[it]

    near = [d * k for k in range(last - FAR, 0, -1) for d in (1, -1)]
    far = [last] + [d * k for k in range(last - 1, last - FAR, -1) for d in (1, -1)]
    far_places = [
        (far.index(d if d == last else -d) * NY + (-k) % NY, (lax.rem(z + d + nz, nz) * NY + lax.rem(y + k, NY), me_c))
        for d in far for k in (2, 1, 3, 0)
    ]
    near_places = [(1 + near.index(-d), at_z(d)) for d in near]
    y_places = [(NY - k, at_y(k)) for k in (2, 1, 3)]

    def over_rows(it, value, combine):
        col_y[it, 0] = value
        mine = col_y.at[it, 0]
        for slot, place in y_places:
            send(mine, col_y.at[it, slot], send_y.at[it], recv_y.at[it], place)
        for slot, place in far_places:
            send(mine, col_far.at[it, slot], send_far.at[it], recv_far.at[it], place)
        wait(col_y.at[it, pl.ds(1, NY - 1)], recv_y.at[it])
        col_near[it, 0] = combine(col_y[it])
        for slot, place in near_places:
            send(col_near.at[it, 0], col_near.at[it, slot], send_near.at[it], recv_near.at[it], place)
        wait(col_far.at[it], recv_far.at[it])
        beyond = combine(col_far[it])
        wait(col_near.at[it, pl.ds(1, len(near))], recv_near.at[it])
        return combine(col_near[it], beyond[None])

    scores = [-dist[:, t] for t in tiles(dcols)]
    top = jnp.max(jnp.maximum(jnp.maximum(scores[0], scores[1]), jnp.maximum(scores[2], scores[3])), axis=1, keepdims=True)
    logs = top + jnp.log(jnp.sum(sum(jnp.exp(score - top) for score in scores), axis=1, keepdims=True))
    logs = jnp.transpose(jnp.broadcast_to(logs, (rows, 128)))[0:1, :]
    u = to_column(-log_noise - logsum(over_cols(0, logs)))

    logs = []
    for t in tiles(dcols):
        scores = u - dist[:, t]
        top = jnp.max(scores, axis=0, keepdims=True)
        logs.append(top + jnp.log(jnp.sum(jnp.exp(scores - top), axis=0, keepdims=True)))
    v = -log_data - over_rows(0, jnp.concatenate(logs, axis=1), logsum)

    def shifted(u, v):
        return [jnp.exp(u + v[:, t] - dist[:, t]) for t in tiles(dcols)]

    for it in (1, 2):
        total = plainsum(over_cols(it, sum_lanes(sum(shifted(u, v)))))
        u = u - to_column(log_noise + jnp.log(total))
        total = jnp.concatenate([jnp.sum(part, axis=0, keepdims=True) for part in shifted(u, v)], axis=1)
        v = v - (log_data + jnp.log(over_rows(it, total, plainsum)))

    total = jnp.zeros((rows, 128), F32)
    for t in tiles(dcols):
        part = jnp.exp(u + v[:, t] - dist[:, t] + log_noise)
        total += part
        out_ref[:, t] = part.astype(BF16)

    def share(c, first=0, width=feats):
        d = gathered[pl.ds(pl.multiple_of(c * feats + first, 16), width), :]
        return lax.dot_general(out_ref[...], d, NT, preferred_element_type=F32)

    def other(k):
        sib_out[k] = share(lax.rem(x + k, NX) * 2 + 1 - core).astype(BF16)
        send(sib_out.at[k], sib_in.at[k], send_sib, recv_sib.at[k], sibling)

    def both(k):
        block = share(lax.rem(x + k, NX) * 2 + core)
        wait(sib_in.at[k], recv_sib.at[k])
        return block + sib_in[k].astype(F32)

    across = lax.rem(x + 2, NX) * 2
    halves = (slice(0, fhalf), slice(fhalf, feats))
    for h, f in enumerate(halves):
        sib_out[2, :, f] = share(across + 1 - core, h * fhalf, fhalf).astype(BF16)
        send(sib_out.at[2, :, f], sib_in.at[2, :, f], send_sib, recv_sib.at[2 + 2 * h], sibling)
    for h, f in enumerate(halves):
        block = share(across + core, h * fhalf, fhalf)
        wait(sib_in.at[2, :, f], recv_sib.at[2 + 2 * h])
        pair[2 + 3 * h] = (block + sib_in[2, :, f].astype(F32)).astype(BF16)
        send(pair.at[2 + 3 * h], relay.at[h], send_x, recv_relay.at[h], at_x(1 - 2 * h))
    other(1)
    right = both(1)
    pair[1] = right[:, fhalf:].astype(BF16)
    send(pair.at[1], inbox.at[1], send_x, recv_in.at[1], at_x(1))
    other(3)
    left = both(3)
    pair[3] = left[:, :fhalf].astype(BF16)
    send(pair.at[3], inbox.at[2], send_x, recv_in.at[2], at_x(-1))
    row_box[3, 0] = sum_lanes(total)
    for k in range(1, nc):
        send(row_box.at[3, 0], row_box.at[3, nc - k], send_row.at[3], recv_row.at[3], at_c(k))
    other(0)
    wait(relay.at[0], recv_relay.at[0])
    pair[0] = (right[:, :fhalf] + relay[0].astype(F32)).astype(BF16)
    send(pair.at[0], inbox.at[0], send_x, recv_in.at[0], at_x(1))
    wait(relay.at[1], recv_relay.at[1])
    pair[4] = (left[:, fhalf:] + relay[1].astype(F32)).astype(BF16)
    send(pair.at[4], inbox.at[3], send_x, recv_in.at[3], at_x(-1))
    own[...] = both(0)
    row_left(2)
    col_left(2)
    wait(row_box.at[3, pl.ds(1, nc - 1)], recv_row.at[3])
    scale = to_column(1.0 / jnp.sum(row_box[3], axis=0))
    row_left(3)
    wait(sib_out, send_sib)
    for i in (1, 2, 0, 3):
        wait(inbox.at[i], recv_in.at[i])
    for first, i, k in ((0, 0, 2), (fhalf, 1, 3)):
        for t in tiles(fhalf):
            f = slice(first + t.start, first + t.stop)
            block = own[:, f] + inbox[i, :, t].astype(F32) + inbox[k, :, t].astype(F32)
            out_ref[:, f] = (block * scale).astype(BF16)
    wait(pair, send_x)


def solution(mesh):
    nz = mesh.shape["rows"] // NY
    nc = mesh.shape["cols"]

    def shards(noise, data):
        data = data.T
        rows, feats = noise.shape
        depth, dcols = data.shape
        dma = pltpu.SemaphoreType.DMA
        vmem = pl.BlockSpec(memory_space=pltpu.VMEM)

        def body(*refs):
            kernel(nz, *refs)

        return pl.pallas_call(
            body,
            out_shape=jax.ShapeDtypeStruct((rows, feats), BF16),
            in_specs=[pl.BlockSpec(memory_space=pl.ANY)] * 2,
            out_specs=vmem,
            scratch_shapes=[
                pltpu.VMEM((FEATURES, dcols), BF16),
                pltpu.VMEM((nc, rows, feats), BF16),
                pltpu.VMEM((rows, dcols), F32),
                pltpu.VMEM((1, dcols), F32),
                pltpu.VMEM((rows, 128), F32),
                pltpu.VMEM((4, nc, 1, rows), F32),
                pltpu.VMEM((3, NY, 1, dcols), F32),
                pltpu.VMEM((3, nz - 2 * FAR + 1, 1, dcols), F32),
                pltpu.VMEM((3, (2 * FAR - 1) * NY, 1, dcols), F32),
                pltpu.VMEM((NX, rows, feats), BF16),
                pltpu.VMEM((NX, rows, feats), BF16),
                pltpu.VMEM((6, rows, feats // 2), BF16),
                pltpu.VMEM((2, rows, feats // 2), BF16),
                pltpu.VMEM((4, rows, feats // 2), BF16),
                pltpu.VMEM((rows, feats), F32),
                dma((2,)), dma((nz * NY,)), dma((nz * NY * 2,)), dma((nz * 2,)), dma((nc,)),
                dma((4,)), dma((3,)), dma((3,)), dma((3,)), dma((NX + 1,)), dma((2,)), dma((4,)),
                dma, dma, dma, dma, dma, dma, dma((4,)), dma((3,)), dma((3,)), dma((3,)), dma, dma,
            ],
            compiler_params=pltpu.CompilerParams(
                collective_id=0, has_side_effects=True, vmem_limit_bytes=54784 * 2**10
            ),
        )(noise, data)

    return jax.shard_map(
        shards,
        mesh=mesh,
        in_specs=(P("rows", "cols"), P("cols", "rows")),
        out_specs=P("rows", "cols"),
        check_vma=False,
    )
```
